128 devices in a mesh: ctx: 32 (over y, x, core), wt: 2 (over z_hi), seq: 2 (over z_lo).
Axes of the slice: x: 4, y: 4, z: 4 (z_hi: 2, z_lo: 2; z = z_hi * 2 + z_lo), core: 2. Of those that a mesh axis runs over, the one named last changes fastest.
Arguments:
- tokens: bfloat16 [4, 4096, 1536], P(('wt', 'seq'), 'ctx'), may hold values from -6 to 6
- cotangent: bfloat16 [4, 4096, 1536], P(('wt', 'seq'), 'ctx'), may hold values from -6 to 6
- segment_ids: int32 [4, 4096], P(('wt', 'seq'), 'ctx'), may hold values from 0 to 4095, as said below
- routes: int32 [4, 4096, 6], P(('wt', 'seq'), 'ctx'), may hold values from 0 to 31, all different within a row; in each aligned block of 128 rows (0 to 127, 128 to 255, ..., all dimensions but the last counted through in order) at most 48 rows name the same one
- gates: float32 [4, 4096, 6], P(('wt', 'seq'), 'ctx'), may hold values from 0.3 to 1
- dense_weights: float32 [1536, 7168], P(('ctx', 'wt', 'seq'))
- dense_first: float32 [1536, 7168], P(('ctx', 'wt', 'seq')), may hold values from -0.00015258789 to 0.00015258789
- dense_second: float32 [1536, 7168], P(('ctx', 'wt', 'seq')), may hold values from 3.2110246e-09 to 1.2844098e-08
- expert_weights: float32 [32, 1536, 1536], P('ctx', ('wt', 'seq'))
- expert_first: float32 [32, 1536, 1536], P('ctx', ('wt', 'seq')), may hold values from -3.8146973e-05 to 3.8146973e-05
- expert_second: float32 [32, 1536, 1536], P('ctx', ('wt', 'seq')), may hold values from 1.9266148e-10 to 7.7064594e-10
- gains: float32 [2, 1536], replicated
- gain_first: float32 [2, 1536], P(None, ('ctx', 'wt', 'seq')), may hold values from -0.00036621094 to 0.00036621094
- gain_second: float32 [2, 1536], P(None, ('ctx', 'wt', 'seq')), may hold values from 1.4128508e-08 to 5.7798445e-08
Outputs:
- block_out: bfloat16 [4, 4096, 1536], P(('wt', 'seq'), 'ctx')
- input_grad: float32 [4, 4096, 1536], P(('wt', 'seq'), 'ctx')
- grad_norm: float32 [], replicated
- dense_new: float32 [1536, 7168], P(('ctx', 'wt', 'seq'))
- dense_first_new: float32 [1536, 7168], P(('ctx', 'wt', 'seq'))
- dense_second_new: float32 [1536, 7168], P(('ctx', 'wt', 'seq'))
- expert_new: float32 [32, 1536, 1536], P('ctx', ('wt', 'seq'))
- expert_first_new: float32 [32, 1536, 1536], P('ctx', ('wt', 'seq'))
- expert_second_new: float32 [32, 1536, 1536], P('ctx', ('wt', 'seq'))
- gain_new: float32 [2, 1536], P(None, ('ctx', 'wt', 'seq'))
- gain_first_new: float32 [2, 1536], P(None, ('ctx', 'wt', 'seq'))
- gain_second_new: float32 [2, 1536], P(None, ('ctx', 'wt', 'seq'))
The draws below stay inside these ranges and needn't reach their ends.
Inputs may be any that keep to these rules, and one draw needn't show every extreme that they name: `segment_ids`: document numbers start at 0 and never fall along a sequence; the last document of each sequence has the number 4096 - 1. A token's 6 experts differ; in each aligned block of 128 positions (the positions of one index of ctx) no expert is named by more than 48 routes, a bound that some block reaches.
All inputs are finite; a program needn't handle non-finite values.
Results may differ from the reference program's by a relative error of at most 0.02.
Values may be sent and summed in bfloat16 or wider, within the bound.
No kernel may reach another device: no remote copies, remote signals or barrier semaphores. Data moves between devices by JAX's collectives and lax.ppermute only.
A program may use at most 256 MiB of HBM per device.

```python
import math
import jax
import jax.numpy as jnp
import numpy as np
from jax import lax

D = 1536
HEADS = 12
KV_HEADS = 4
HEAD_DIM = 128
EXPERT_FF = 512
SHARED_FF = 1024
TOP = 6
TOK_DEV = 128
STEP = 10
EXPERTS = 32
CAP = 48
SEQ_LEN = 4096
SEQS = 4
DCOLS = 7168
N_CTX = 32


def dense_scales():
    columns = jnp.arange(DCOLS)
    query_width = HEADS * HEAD_DIM
    kv_width = KV_HEADS * HEAD_DIM
    output_start = query_width + 2 * kv_width
    shared_start = output_start + query_width
    down_start = shared_start + 2 * SHARED_FF
    scales = jnp.where(columns < output_start, D ** (-0.5), SHARED_FF ** (-0.5))
    scales = jnp.where((columns >= output_start) & (columns < shared_start), 4.0 * query_width ** (-0.5), scales)
    scales = jnp.where((columns >= shared_start) & (columns < down_start), D ** (-0.5), scales)
    return scales.astype(jnp.float32)


def expert_scales():
    columns = jnp.arange(3 * EXPERT_FF)
    scales = jnp.where(columns < 2 * EXPERT_FF, D ** (-0.5), EXPERT_FF ** (-0.5))
    return scales.astype(jnp.float32)


def draw_segment_ids(key, part):
    key = jax.random.fold_in(key, 11)
    key_start, key_end, key_cuts = jax.random.split(key, 3)
    first_start = jax.random.randint(key_start, (SEQS, 1), 0, TOK_DEV)
    long_end = jax.random.randint(key_end, (SEQS, 1), SEQ_LEN - TOK_DEV, SEQ_LEN - 1)
    places = jnp.arange(SEQ_LEN, dtype=jnp.int32)[None, :]
    cuts = jax.random.randint(key_cuts, (SEQS, SEQ_LEN), 0, 16) == 0
    outside = (places < first_start) | (places > long_end)
    starts = cuts & outside | (places == first_start) | (places == long_end + 1)
    starts = starts & (places > 0)
    counted = jnp.cumsum(starts.astype(jnp.int32), axis=1).astype(jnp.int32)
    return jnp.where(places > long_end, SEQ_LEN - 1, counted).astype(jnp.int32)


def draw_dense_weights(key, part):
    key = jax.random.fold_in(key, 21)
    base = jax.random.normal(key, (D, DCOLS), jnp.float32)
    return (base * dense_scales()[None, :]).astype(jnp.float32)


def draw_expert_weights(key, part):
    key = jax.random.fold_in(key, 31)
    base = jax.random.normal(key, (EXPERTS, D, 3 * EXPERT_FF), jnp.float32)
    return (base * expert_scales()[None, None, :]).astype(jnp.float32)


def draw_gains(key, part):
    key = jax.random.fold_in(key, 41)
    spots = jnp.arange(D, dtype=jnp.float32) / (D - 1)
    noise = jax.random.uniform(key, (2, D), jnp.float32, -1.0, 1.0)
    rising = 0.6 * (1.0 + 2.0 * spots)
    return (rising[None, :] * (1.0 + 0.15 * noise)).astype(jnp.float32)


def steps_of(own_key, shape, shards, low, top_value):
    loudness, own = 1.0, jax.random.fold_in(own_key, 6)
    for axis_at, parts in shards:
        draws = jnp.exp(jax.random.uniform(jax.random.fold_in(own, axis_at), (parts,), jnp.float32, low / len(shards), top_value / len(shards)))
        loudness = loudness * jnp.repeat(draws, shape[axis_at] // parts).reshape([-1 if axis == axis_at else 1 for axis in range(len(shape))])
    return loudness


def deal_out(rng, own, number, rows, number_of, top, most, lean):
    order = jax.random.permutation(rng, number_of)
    heavy_load, common = portions_of(number_of, rows * top, most, lean, True), portions_of(number_of, rows * top, most, lean, False)
    places = jnp.arange(number_of)

    def named(sizes, offset_by):
        used = int((sizes > 0).sum())
        fixed = max(1, used // 4)
        moved = fixed + (places - fixed + offset_by * (used - fixed)) % max(1, number_of - fixed)
        return jnp.zeros((number_of,), jnp.int32).at[order[jnp.where(places < fixed, places, moved)]].set(jnp.asarray(sizes, jnp.int32))

    sizes = jnp.where(number % 4 == 0, named(heavy_load, number // 4), named(common, number - number // 4 - 1))
    mixed = jax.random.permutation(jax.random.fold_in(own, 3), number_of)
    donor, receiver = mixed[0:number_of // 2 * 2:2], mixed[1:number_of // 2 * 2:2]
    room = jnp.minimum(sizes[donor] - 1, most - sizes[receiver]) // 2
    room = jnp.where((donor == order[0]) | (receiver == order[0]) | (sizes[receiver] == 0), 0, jnp.maximum(room, 0))
    moved = jax.random.randint(jax.random.fold_in(own, 4), (number_of // 2,), 0, 1 << 20) % (room + 1)
    sizes = sizes.at[donor].add(-moved).at[receiver].add(moved)
    items = jnp.searchsorted(jnp.cumsum(sizes), jnp.arange(rows * top), side="right").astype(jnp.int32)
    listing = items.reshape(top, rows).T
    listing = listing[jax.random.permutation(jax.random.fold_in(own, 1), rows)]
    offset_by = jax.random.randint(jax.random.fold_in(own, 2), (rows, 1), 0, top)
    return jnp.take_along_axis(listing, (jnp.arange(top)[None, :] + offset_by) % top, axis=1)


def portions_of(amount, total, limit, lean, full):
    portions = [(1 << 20) // math.isqrt(standing ** lean) + 1 for standing in range(1, amount + 1)]
    largest = limit if full else min(limit, max(-(-total // amount), total * portions[0] // sum(portions)))
    least = 1 if total - largest >= amount - 1 else 0
    given, rest = [largest] + [least] * (amount - 1), total - largest - least * (amount - 1)
    while rest > 0:
        movable = [i for i in range(1, amount) if given[i] < largest] or [i for i in range(1, amount) if given[i] < limit]
        pool, left = sum([portions[i] for i in movable]), rest
        for i in movable:
            extra = min(limit - given[i], max(1, left * portions[i] // pool), rest)
            given[i] = given[i] + extra
            rest = rest - extra
    return np.array(given)


def scatter_about(key, dims, scale, bound, cuts=(), held_as=jnp.bfloat16):
    drawn = scale * jax.random.normal(key, dims, jnp.float32)
    if cuts:
        drawn = drawn * steps_of(key, dims, cuts, -0.22, 0.18)
    return jnp.clip(drawn, -bound, bound).astype(held_as)


def setup_inputs(seed: int = 0) -> dict:
    splits = jax.random.split(jax.random.key(seed), 15)
    tokens = scatter_about(splits[0], (SEQS, SEQ_LEN, D), 1.0, 6.0, ((0, 4), (1, 32)))
    cotangent = scatter_about(splits[1], (SEQS, SEQ_LEN, D), 1.0, 6.0, ((0, 4), (1, 32)))
    segment_ids = draw_segment_ids(jax.random.fold_in(splits[14], 71), 0)
    routes_keys = jax.random.split(jax.random.fold_in(splits[3], 1), SEQS * SEQ_LEN // TOK_DEV)
    routes_turns = jax.random.permutation(jax.random.fold_in(splits[3], 3), SEQS * SEQ_LEN // TOK_DEV)
    routes = jax.vmap(lambda own, number: deal_out(jax.random.fold_in(splits[3], 2), own, number, TOK_DEV, EXPERTS, TOP, CAP, 1))(routes_keys, routes_turns).reshape((SEQS, SEQ_LEN, TOP))
    gates = jnp.clip(0.3 + 0.7 * jax.random.uniform(splits[4], (SEQS, SEQ_LEN, TOP), jnp.float32) ** steps_of(splits[4], (SEQS, SEQ_LEN, TOP), ((0, 4), (1, 32)), -0.2, 0.2), 0.3, 1.0)
    dense_weights = draw_dense_weights(jax.random.fold_in(splits[14], 71), 0)
    dense_first = scatter_about(splits[6], (D, DCOLS), (0.077 * (0.5 * D * DCOLS + 2.9 * D * EXPERT_FF) ** -0.5), 0.00015258789, ((0, 128),), jnp.float32)
    dense_second = jnp.clip(jnp.exp(math.log(1.284409822943644e-08) - 1.3862944 * jax.random.uniform(splits[7], (D, DCOLS), jnp.float32) ** steps_of(splits[7], (D, DCOLS), ((0, 128),), -0.2, 0.2)), 3.21102455735911e-09, 1.284409822943644e-08)
    expert_weights = draw_expert_weights(jax.random.fold_in(splits[14], 71), 0)
    expert_first = scatter_about(splits[9], (EXPERTS, D, 3 * EXPERT_FF), (0.044 * (TOP * EXPERTS ** -1) ** 0.5 * (0.5 * D * DCOLS + 2.9 * D * EXPERT_FF) ** -0.5), 3.814697265625e-05, ((0, 32), (1, 4)), jnp.float32)
    expert_second = jnp.clip(jnp.exp(math.log(7.706459359546614e-10) - 1.3862944 * jax.random.uniform(splits[10], (EXPERTS, D, 3 * EXPERT_FF), jnp.float32) ** steps_of(splits[10], (EXPERTS, D, 3 * EXPERT_FF), ((0, 32), (1, 4)), -0.2, 0.2)), 1.9266148398866534e-10, 7.706459359546614e-10)
    gains = draw_gains(jax.random.fold_in(splits[14], 71), 0)
    gain_first = scatter_about(splits[12], (2, D), (0.165 * (0.5 * D * DCOLS + 2.9 * D * EXPERT_FF) ** -0.5), 0.00036621094, ((1, 128),), jnp.float32)
    gain_second = jnp.clip(jnp.exp(math.log(5.779844514108845e-08) - 1.40876726 * jax.random.uniform(splits[13], (2, D), jnp.float32) ** steps_of(splits[13], (2, D), ((1, 128),), -0.2, 0.2)), 1.4128508141197926e-08, 5.779844514108845e-08)
    return dict(tokens=tokens, cotangent=cotangent, segment_ids=segment_ids, routes=routes, gates=gates, dense_weights=dense_weights, dense_first=dense_first, dense_second=dense_second, expert_weights=expert_weights, expert_first=expert_first, expert_second=expert_second, gains=gains, gain_first=gain_first, gain_second=gain_second)


EPS_NORM = 1e-05
CLIP_NORM = 1.0
FIRST_DECAY = 0.9
SECOND_DECAY = 0.95
ADAM_EPS = 1e-08
WEIGHT_DECAY = 0.1
MATRIX_RATE = 0.05
GAIN_RATE = 0.6
NEGATIVE = -1e+30
PRECISE = lax.Precision.HIGHEST

@jax.custom_vjp
def low(v):
    return lax.optimization_barrier(v.astype(jnp.bfloat16)).astype(jnp.float32)

@jax.custom_vjp
def low_back(v):
    return v

def low_keep(v):
    return (low(v), None)

def low_pass(kept, grad):
    return (grad,)

def back_keep(v):
    return (v, None)

def back_low(kept, grad):
    return (low(grad),)
low.defvjp(low_keep, low_pass)
low_back.defvjp(back_keep, back_low)

def rms_norm(values, gain_row):
    factor = lax.rsqrt(lax.optimization_barrier(jnp.mean(values * values, axis=-1, keepdims=True)) + EPS_NORM)
    return values * factor * gain_row

@jax.checkpoint
def attend_block(query_block, spots, labels, key_heads, value_heads, places, segments):
    scores = jnp.einsum('qhgd,shd->hgqs', query_block, key_heads, precision=PRECISE) * HEAD_DIM ** (-0.5)
    scores = low_back(scores)
    visible = (labels[:, None] == segments[None, :]) & (places[None, :] <= spots[:, None])
    scores = jnp.where(visible[None, None], scores, NEGATIVE)
    weights = low(jax.nn.softmax(scores, axis=-1))
    result = jnp.einsum('hgqs,shd->qhgd', weights, value_heads, precision=PRECISE)
    return result.reshape(spots.shape[0], HEADS * HEAD_DIM)

def attend(query, keys, values, segments):
    group_size = HEADS // KV_HEADS
    block_rows = min(512, SEQ_LEN)
    block_count = SEQ_LEN // block_rows
    places = jnp.arange(SEQ_LEN, dtype=jnp.int32)
    key_heads = keys.reshape(SEQ_LEN, KV_HEADS, HEAD_DIM)
    value_heads = values.reshape(SEQ_LEN, KV_HEADS, HEAD_DIM)
    query_blocks = query.reshape(block_count, block_rows, KV_HEADS, group_size, HEAD_DIM)
    spot_blocks = places.reshape(block_count, block_rows)
    label_blocks = segments.reshape(block_count, block_rows)

    def one_block(items):
        return attend_block(items[0], items[1], items[2], key_heads, value_heads, places, segments)
    results = lax.map(one_block, (query_blocks, spot_blocks, label_blocks))
    return results.reshape(SEQ_LEN, HEADS * HEAD_DIM)

def expert_slots(route_rows):
    flat = route_rows.reshape(N_CTX, TOK_DEV * TOP)
    labels = jnp.arange(EXPERTS, dtype=jnp.int32)
    onehot = (flat[:, :, None] == labels[None, None, :]).astype(jnp.int32)
    before = jnp.cumsum(onehot, axis=1) - onehot
    slot_index = lax.optimization_barrier(jnp.sum(before * onehot, axis=2))
    row_index = slot_index + (jnp.arange(N_CTX, dtype=jnp.int32) * CAP)[:, None]
    return (flat.reshape(-1), row_index.reshape(-1))

def forward(inputs, dense, experts, gain_rows, segments, route_rows, gate_rows):
    query_width = HEADS * HEAD_DIM
    kv_width = KV_HEADS * HEAD_DIM
    qkv_end = query_width + 2 * kv_width
    shared_start = qkv_end + query_width
    down_start = shared_start + 2 * SHARED_FF
    dense_low = low(dense)
    h_one = low(rms_norm(inputs, gain_rows[0]))
    query = low(low_back(jnp.dot(h_one, dense_low[:, :query_width], precision=PRECISE)))
    keys = low(low_back(jnp.dot(h_one, dense_low[:, query_width:query_width + kv_width], precision=PRECISE)))
    values = low(low_back(jnp.dot(h_one, dense_low[:, query_width + kv_width:qkv_end], precision=PRECISE)))
    attn = low(low_back(attend(query, keys, values, segments)))
    resid = inputs + low_back(jnp.dot(attn, dense_low[:, qkv_end:shared_start].T, precision=PRECISE))
    h_two = low(rms_norm(resid, gain_rows[1]))
    shared_gate = low_back(jnp.dot(h_two, dense_low[:, shared_start:shared_start + SHARED_FF], precision=PRECISE))
    shared_up = low_back(jnp.dot(h_two, dense_low[:, shared_start + SHARED_FF:down_start], precision=PRECISE))
    shared_mid = low(jax.nn.silu(shared_gate) * shared_up)
    shared_out = jnp.dot(shared_mid, dense_low[:, down_start:].T, precision=PRECISE)
    expert_flat, row_flat = expert_slots(route_rows)
    token_flat = jnp.arange(SEQ_LEN * TOP, dtype=jnp.int32) // TOP
    buffer = jnp.zeros((EXPERTS, N_CTX * CAP, D), h_two.dtype).at[expert_flat, row_flat].set(h_two[token_flat])
    experts_low = low(experts)
    gate_pre = low_back(jnp.einsum('erd,edf->erf', buffer, experts_low[:, :, :EXPERT_FF], precision=PRECISE))
    up_pre = low_back(jnp.einsum('erd,edf->erf', buffer, experts_low[:, :, EXPERT_FF:2 * EXPERT_FF], precision=PRECISE))
    expert_mid = low(jax.nn.silu(gate_pre) * up_pre)
    expert_out = low(low_back(jnp.einsum('erf,edf->erd', expert_mid, experts_low[:, :, 2 * EXPERT_FF:], precision=PRECISE)))
    picked = expert_out[expert_flat, row_flat].reshape(SEQ_LEN, TOP, D)
    mixture = lax.optimization_barrier(jnp.sum(gate_rows[:, :, None] * picked, axis=1))
    return resid + shared_out + mixture

def adamw_step(weight, first_moment, second, gradient, step_rate, decay_rate):
    first_moment = FIRST_DECAY * first_moment + (1.0 - FIRST_DECAY) * gradient
    second = SECOND_DECAY * second + (1.0 - SECOND_DECAY) * gradient * gradient
    first_hat = first_moment / (1.0 - FIRST_DECAY ** STEP)
    second_hat = second / (1.0 - SECOND_DECAY ** STEP)
    weight = weight - step_rate * (first_hat / (jnp.sqrt(second_hat) + ADAM_EPS) + decay_rate * weight)
    return (weight, first_moment, second)

def reference(tokens, cotangent, segment_ids, routes, gates, dense_weights, dense_first, dense_second, expert_weights, expert_first, expert_second, gains, gain_first, gain_second):

    def per_sequence(carry, items):
        inputs, upstream, segments, route_rows, gate_rows = items

        def layer(inputs_f, dense, experts, gain_rows):
            return forward(inputs_f, dense, experts, gain_rows, segments, route_rows, gate_rows)
        result, pull = jax.vjp(layer, inputs.astype(jnp.float32), dense_weights, expert_weights, gains)
        d_inputs, d_dense, d_experts, d_gains = pull(upstream.astype(jnp.float32))
        carry = (carry[0] + d_dense, carry[1] + d_experts, carry[2] + d_gains)
        return (carry, (result.astype(jnp.bfloat16), d_inputs))
    start = (jnp.zeros_like(dense_weights), jnp.zeros_like(expert_weights), jnp.zeros_like(gains))
    totals, outputs = lax.scan(per_sequence, start, (tokens, cotangent, segment_ids, routes, gates))
    grad_dense, grad_experts, grad_gains = totals
    block_out, input_grad = outputs
    squares = jnp.sum(grad_dense * grad_dense) + jnp.sum(grad_experts * grad_experts) + jnp.sum(grad_gains * grad_gains)
    grad_norm = jnp.sqrt(squares)
    clip_factor = jnp.minimum(1.0, CLIP_NORM / (grad_norm + 1e-06))
    dense_new, dense_first_new, dense_second_new = adamw_step(dense_weights, dense_first, dense_second, grad_dense * clip_factor, MATRIX_RATE, WEIGHT_DECAY)
    expert_new, expert_first_new, expert_second_new = adamw_step(expert_weights, expert_first, expert_second, grad_experts * clip_factor, MATRIX_RATE, WEIGHT_DECAY)
    gain_new, gain_first_new, gain_second_new = adamw_step(gains, gain_first, gain_second, grad_gains * clip_factor, GAIN_RATE, 0.0)
    return (block_out, input_grad, grad_norm, dense_new, dense_first_new, dense_second_new, expert_new, expert_first_new, expert_second_new, gain_new, gain_first_new, gain_second_new)
```

```python
import functools

import jax
import jax.numpy as jnp
from jax import lax
from jax.experimental import pallas as pl
from jax.experimental.layout import Layout, with_layout_constraint
from jax.experimental.pallas import tpu as pltpu
from jax.sharding import Mesh
from jax.sharding import PartitionSpec as P

HEADS = 12
KV_HEADS = 4
HEAD_DIM = 128
GROUP = HEADS // KV_HEADS
EXPERT_FF = 512
SHARED_FF = 1024
TOP = 6
STEP = 10

EPS_NORM = 1e-05
CLIP_NORM = 1.0
FIRST_DECAY = 0.9
SECOND_DECAY = 0.95
ADAM_EPS = 1e-08
WEIGHT_DECAY = 0.1
MATRIX_RATE = 0.05
GAIN_RATE = 0.6
NEGATIVE = -1e30

QW = HEADS * HEAD_DIM
KW = KV_HEADS * HEAD_DIM
STARTS = (0, QW, QW + KW, QW + 2 * KW, 2 * QW + 2 * KW, 2 * QW + 2 * KW + SHARED_FF, 2 * QW + 2 * KW + 2 * SHARED_FF)
WIDTHS = (QW, KW, KW, QW, SHARED_FF, SHARED_FF, SHARED_FF)
HALF_WIDTHS = tuple(w // 2 for w in WIDTHS)
HALF_COLS = sum(HALF_WIDTHS)
QKV_HALF = sum(HALF_WIDTHS[:3])
HEADS_HALF = HEADS // 2
KV_HALF = KV_HEADS // 2

CHIPS = ("y", "x")
CTX = ("y", "x", "core")
DEPTH = ("wt", "seq")
COLUMN = ("core", "wt", "seq")
ALL = CTX + DEPTH
BF = jnp.bfloat16
F32 = jnp.float32
LOG2E = 1.4426950408889634
VMEM_LIMIT = 48 << 20


def turn(v, phase, step):
    pairs = []
    for y in range(4):
        for x in range(4):
            for core in range(2):
                along_x = (phase == 1) == (core == 0)
                ty, tx = (y, (x + step) % 4) if along_x else ((y + step) % 4, x)
                pairs.append(((y * 4 + x) * 2 + core, (ty * 4 + tx) * 2 + core))
    return lax.ppermute(v, CTX, pairs)


def swap(v):
    return lax.ppermute(v, "core", [(0, 1), (1, 0)])


def middle(rows):
    return (rows // 2 + 7) // 8 * 8


def ring_gather(v, phase):
    left = turn(v, phase, 1)
    right = turn(v, phase, -1)
    half = middle(v.shape[0])
    far_a = turn(left[:half], phase, 1)
    far_b = turn(right[half:], phase, -1)
    return jnp.concatenate([v, left, right, far_a, far_b], axis=0)


def gather_plane(v):
    return ring_gather(ring_gather(v, 1), 2)


def ring_sum(g, phase):
    rows = g.shape[0] // 4
    own, left, right, far = (g[k * rows : (k + 1) * rows] for k in range(4))
    half = middle(rows)
    from_left = turn(far[:half], phase, 1)
    from_right = turn(far[half:], phase, -1)
    to_right = jnp.concatenate(
        [(right[:half].astype(F32) + from_left.astype(F32)).astype(BF), right[half:]], axis=0
    )
    to_left = jnp.concatenate(
        [left[:half], (left[half:].astype(F32) + from_right.astype(F32)).astype(BF)], axis=0
    )
    one = turn(to_right, phase, 1)
    two = turn(to_left, phase, -1)
    return own.astype(F32) + one.astype(F32) + two.astype(F32)


def sum_plane(g):
    return ring_sum(ring_sum(g, 2).astype(BF), 1)


def block_chips(iy, ix, first_core):
    offsets = jnp.array([0, 3, 1, 2], jnp.int32)
    outer, inner = jnp.repeat(offsets, 4), jnp.tile(offsets, 4)
    y = (iy + jnp.where(first_core, outer, inner)) % 4
    x = (ix + jnp.where(first_core, inner, outer)) % 4
    return y * 4 + x


def row_major(v):
    return with_layout_constraint(v, Layout(tuple(range(v.ndim))))


def attend_kernel(scale, kpos_ref, qpos_ref, q_ref, kv_ref, out_ref, lse_ref, acc, top, total):
    step = pl.program_id(0)

    @pl.when(step == 0)
    def _():
        acc[...] = jnp.zeros_like(acc)
        total[...] = jnp.zeros_like(total)
        top[...] = jnp.full_like(top, -jnp.inf)

    spots = kpos_ref[...]
    visible = (spots >= qpos_ref[0:1, :]) & (spots <= qpos_ref[1:2, :])
    for head in range(HEADS_HALF):
        kv_head = head // GROUP
        cols = slice(head * HEAD_DIM, (head + 1) * HEAD_DIM)
        key = kv_ref[:, kv_head * HEAD_DIM : (kv_head + 1) * HEAD_DIM]
        value = kv_ref[:, (KV_HALF + kv_head) * HEAD_DIM : (KV_HALF + kv_head + 1) * HEAD_DIM]
        scores = times_transposed(key, q_ref[:, cols]) * (scale * LOG2E)
        scores = jnp.where(visible, scores, NEGATIVE)
        before = top[head : head + 1, :]
        now = jnp.maximum(before, jnp.max(scores, axis=0, keepdims=True))
        expo = jnp.exp2(scores - now)
        fade = jnp.exp2(before - now)
        top[head : head + 1, :] = now
        total[head : head + 1, :] = total[head : head + 1, :] * fade + jnp.sum(
            expo, axis=0, keepdims=True
        )
        acc[cols, :] = acc[cols, :] * fade + transposed_times(value, expo.astype(BF))

    @pl.when(step == pl.num_programs(0) - 1)
    def _():
        for head in range(HEADS_HALF):
            cols = slice(head * HEAD_DIM, (head + 1) * HEAD_DIM)
            out_ref[:, cols] = (acc[cols, :] / total[head : head + 1, :]).T
        lse_ref[...] = top[...] + jnp.log2(total[...])


def attend(key_spots, query_range, query, kv_all, scale):
    rows, cols = query.shape
    keys = kv_all.shape[0]
    block = 512
    return pl.pallas_call(
        functools.partial(attend_kernel, scale),
        grid=(keys // block,),
        in_specs=[
            pl.BlockSpec((block, 1), lambda j: (j, 0)),
            pl.BlockSpec((8, rows), lambda j: (0, 0)),
            pl.BlockSpec((rows, cols), lambda j: (0, 0)),
            pl.BlockSpec((block, kv_all.shape[1]), lambda j: (j, 0)),
        ],
        out_specs=[
            pl.BlockSpec((rows, cols), lambda j: (0, 0)),
            pl.BlockSpec((8, rows), lambda j: (0, 0)),
        ],
        out_shape=[
            jax.ShapeDtypeStruct((rows, cols), F32),
            jax.ShapeDtypeStruct((8, rows), F32),
        ],
        scratch_shapes=[
            pltpu.VMEM((cols, rows), F32),
            pltpu.VMEM((8, rows), F32),
            pltpu.VMEM((8, rows), F32),
        ],
        cost_estimate=pl.CostEstimate(
            flops=4 * rows * cols * keys, bytes_accessed=8 << 20, transcendentals=rows * keys * 6
        ),
        compiler_params=pltpu.CompilerParams(vmem_limit_bytes=VMEM_LIMIT),
    )(key_spots, query_range, query, kv_all)


def attend_back_kernel(
    scale, kpos_ref, qpos_ref, q_ref, do_ref, lse_ref, delta_ref, kv_ref, dq_ref, dkv_ref, acc
):
    step = pl.program_id(0)

    @pl.when(step == 0)
    def _():
        acc[...] = jnp.zeros_like(acc)

    spots = kpos_ref[...]
    visible = (spots >= qpos_ref[0:1, :]) & (spots <= qpos_ref[1:2, :])
    for kv_head in range(KV_HALF):
        k_cols = slice(kv_head * HEAD_DIM, (kv_head + 1) * HEAD_DIM)
        v_cols = slice((KV_HALF + kv_head) * HEAD_DIM, (KV_HALF + kv_head + 1) * HEAD_DIM)
        key, value = kv_ref[:, k_cols], kv_ref[:, v_cols]
        key_grad = jnp.zeros(key.shape, F32)
        value_grad = jnp.zeros(key.shape, F32)
        for member in range(GROUP):
            head = kv_head * GROUP + member
            cols = slice(head * HEAD_DIM, (head + 1) * HEAD_DIM)
            query, upstream = q_ref[:, cols], do_ref[:, cols]
            scores = times_transposed(key, query) * (scale * LOG2E)
            scores = jnp.where(visible, scores, NEGATIVE)
            chances = jnp.exp2(scores - lse_ref[head : head + 1, :])
            inner = times_transposed(value, upstream)
            grad_scores = (chances * (inner - delta_ref[head : head + 1, :])).astype(BF)
            value_grad += dot(chances.astype(BF), upstream)
            key_grad += dot(grad_scores, query)
            acc[cols, :] += transposed_times(key, grad_scores)
        dkv_ref[:, k_cols] = (key_grad * scale).astype(BF)
        dkv_ref[:, v_cols] = value_grad.astype(BF)

    @pl.when(step == pl.num_programs(0) - 1)
    def _():
        for head in range(HEADS_HALF):
            cols = slice(head * HEAD_DIM, (head + 1) * HEAD_DIM)
            dq_ref[:, cols] = (acc[cols, :] * scale).T.astype(BF)


def attend_back(key_spots, query_range, query, upstream, lse, delta, kv_all, scale):
    rows, cols = query.shape
    keys, kv_cols = kv_all.shape
    block = 512
    whole = pl.BlockSpec((rows, cols), lambda j: (0, 0))
    stats = pl.BlockSpec((8, rows), lambda j: (0, 0))
    some = pl.BlockSpec((block, kv_cols), lambda j: (j, 0))
    return pl.pallas_call(
        functools.partial(attend_back_kernel, scale),
        grid=(keys // block,),
        in_specs=[
            pl.BlockSpec((block, 1), lambda j: (j, 0)),
            stats,
            whole,
            whole,
            stats,
            stats,
            some,
        ],
        out_specs=[whole, some],
        out_shape=[
            jax.ShapeDtypeStruct((rows, cols), BF),
            jax.ShapeDtypeStruct((keys, kv_cols), BF),
        ],
        scratch_shapes=[pltpu.VMEM((cols, rows), F32)],
        cost_estimate=pl.CostEstimate(
            flops=10 * rows * cols * keys, bytes_accessed=12 << 20, transcendentals=rows * keys * 6
        ),
        compiler_params=pltpu.CompilerParams(vmem_limit_bytes=VMEM_LIMIT),
    )(key_spots, query_range, query, upstream, lse, delta, kv_all)


def pick_kernel(chips_ref, pick_ref, scale_ref, source_ref, out_ref):
    rows = dot(pick_ref[0], source_ref[0]) * scale_ref[0]
    cap = out_ref.shape[2]
    out_ref[0, 0] = rows[:cap].astype(BF)
    out_ref[1, 0] = rows[cap:].astype(BF)


def pick_rows(chips, pick, scale, source):
    blocks, slots, rows = pick.shape
    width = source.shape[2]
    return pl.pallas_call(
        pick_kernel,
        grid_spec=pltpu.PrefetchScalarGridSpec(
            num_scalar_prefetch=1,
            grid=(blocks,),
            in_specs=[
                pl.BlockSpec((1, slots, rows), lambda b, t: (b, 0, 0)),
                pl.BlockSpec((1, slots, 1), lambda b, t: (b, 0, 0)),
                pl.BlockSpec((1, rows, width), lambda b, t: (t[b], 0, 0)),
            ],
            out_specs=pl.BlockSpec((2, 1, slots // 2, width), lambda b, t: (0, b, 0, 0)),
        ),
        out_shape=jax.ShapeDtypeStruct((2, blocks, slots // 2, width), BF),
        cost_estimate=pl.CostEstimate(
            flops=2 * blocks * slots * rows * width, bytes_accessed=12 << 20, transcendentals=0
        ),
        compiler_params=pltpu.CompilerParams(vmem_limit_bytes=VMEM_LIMIT),
    )(chips, pick, scale, source)


def unpick_kernel(pick_ref, scale_ref, rows_ref, out_ref):
    rows = jnp.concatenate([rows_ref[0, 0], rows_ref[1, 0]], axis=0)
    rows = (rows.astype(F32) * scale_ref[0]).astype(BF)
    out_ref[...] = transposed_times(pick_ref[0], rows).astype(BF)


def unpick_rows(pick, scale, given):
    blocks, slots, rows = pick.shape
    width = given.shape[3]
    return pl.pallas_call(
        unpick_kernel,
        grid=(blocks,),
        in_specs=[
            pl.BlockSpec((1, slots, rows), lambda b: (b, 0, 0)),
            pl.BlockSpec((1, slots, 1), lambda b: (b, 0, 0)),
            pl.BlockSpec((2, 1, slots // 2, width), lambda b: (0, b, 0, 0)),
        ],
        out_specs=pl.BlockSpec((rows, width), lambda b: (b, 0)),
        out_shape=jax.ShapeDtypeStruct((blocks * rows, width), BF),
        cost_estimate=pl.CostEstimate(
            flops=2 * blocks * slots * rows * width, bytes_accessed=12 << 20, transcendentals=0
        ),
        compiler_params=pltpu.CompilerParams(vmem_limit_bytes=VMEM_LIMIT),
    )(pick, scale, given)


def total_over_all(v):
    v = v + swap(v)
    for axis in ("x", "y"):
        v = v + lax.ppermute(v, axis, [(i, i ^ 1) for i in range(4)])
        v = v + lax.ppermute(v, axis, [(i, i ^ 3) for i in range(4)])
    for axis in DEPTH:
        v = v + lax.ppermute(v, axis, [(0, 1), (1, 0)])
    return v


def silu_parts(values):
    sigmoid_values = jax.nn.sigmoid(values)
    return (values * sigmoid_values, sigmoid_values * (1.0 + values * (1.0 - sigmoid_values)))


def norm_forward(values, gain_row):
    factor = lax.rsqrt(jnp.mean(values * values, axis=-1, keepdims=True) + EPS_NORM)
    normed = values * factor
    return (normed * gain_row, normed, factor)


def norm_backward(upstream, normed, factor, gain_row):
    scaled = upstream * gain_row
    inward = factor * (scaled - normed * jnp.mean(scaled * normed, axis=-1, keepdims=True))
    return (inward, jnp.sum(upstream * normed, axis=0))


def adamw_step(weight, first_moment, second, gradient, step_rate, decay_rate):
    first_moment = FIRST_DECAY * first_moment + (1.0 - FIRST_DECAY) * gradient
    second = SECOND_DECAY * second + (1.0 - SECOND_DECAY) * gradient * gradient
    first_hat = first_moment / (1.0 - FIRST_DECAY**STEP)
    second_hat = second / (1.0 - SECOND_DECAY**STEP)
    weight = weight - step_rate * (
        first_hat / (jnp.sqrt(second_hat) + ADAM_EPS) + decay_rate * weight
    )
    return (weight, first_moment, second)


def dot(left, right):
    return jnp.dot(left, right, preferred_element_type=F32)


def times_transposed(left, right):
    return lax.dot_general(left, right, (((1,), (1,)), ((), ())), preferred_element_type=F32)


def transposed_times(left, right):
    return lax.dot_general(left, right, (((0,), (0,)), ((), ())), preferred_element_type=F32)


def halves_of(dense):
    parts = []
    for core in range(2):
        parts.append(
            jnp.concatenate(
                [
                    dense[:, s + core * w : s + (core + 1) * w]
                    for s, w in zip(STARTS, HALF_WIDTHS, strict=True)
                ],
                axis=1,
            )
        )
    return parts


def whole_of(half0, half1):
    columns, at = [], 0
    for w in HALF_WIDTHS:
        columns += [half0[:, at : at + w], half1[:, at : at + w]]
        at += w
    return jnp.concatenate(columns, axis=1)


def shards(
    tokens,
    cotangent,
    segment_ids,
    routes,
    gates,
    dense_weights,
    dense_first,
    dense_second,
    expert_weights,
    expert_first,
    expert_second,
    gains,
    gain_first,
    gain_second,
):
    rows = tokens.shape[1]
    width = tokens.shape[2]
    seq_len = rows * 32
    cap = min(rows, 2 * rows * TOP // 32)
    scale = HEAD_DIM ** (-0.5)
    iy, ix, core = lax.axis_index("y"), lax.axis_index("x"), lax.axis_index("core")
    chip = iy * 4 + ix
    first_core = core == 0
    first_of_chip = chip * 2 * rows

    def both_cores(mine, other):
        return jnp.where(
            first_core,
            jnp.concatenate([mine, other], axis=0),
            jnp.concatenate([other, mine], axis=0),
        )

    def of_chip(v):
        return both_cores(v, swap(v))

    def own_rows(v):
        return lax.dynamic_slice_in_dim(v, core * rows, rows, 0)

    def other_rows(v):
        return lax.dynamic_slice_in_dim(v, (1 - core) * rows, rows, 0)

    def summed_for_own(v):
        return own_rows(v) + swap(other_rows(v))

    def three_terms(v):
        high = v.astype(BF)
        rest = v - high.astype(F32)
        mid = rest.astype(BF)
        return [high, mid, (rest - mid.astype(F32)).astype(BF)]

    segments_chip = of_chip(segment_ids[0][None].astype(F32)).reshape(1, 2 * rows)
    digits = jnp.concatenate(
        [jnp.floor(segments_chip / 64.0), segments_chip - 64.0 * jnp.floor(segments_chip / 64.0)],
        axis=0,
    ).astype(BF)
    small = jnp.concatenate(
        [digits.reshape(4, rows), routes[0].T.astype(BF), *three_terms(gates[0].T)], axis=0
    )
    small_rows = small.shape[0]
    small = jnp.pad(small.reshape(-1), (0, 8 * QKV_HALF - small.size)).reshape(8, QKV_HALF)

    dense_low = dense_weights.astype(BF)
    dense_both = jnp.stack(halves_of(dense_low))[:, None]
    dense_both = jnp.broadcast_to(dense_both, (2, 4, *dense_low.shape[:1], HALF_COLS))
    chip_rows = 8 * dense_low.shape[0]
    dense_half = lax.all_to_all(
        dense_both.reshape(8, -1, HALF_COLS), COLUMN, 0, 0, tiled=True
    ).reshape(chip_rows, HALF_COLS)
    chips = block_chips(iy, ix, first_core)
    qkv_all = gather_plane(jnp.concatenate([dense_half[:, :QKV_HALF], small], axis=0))
    qkv_all = qkv_all.reshape(16, chip_rows + 8, QKV_HALF)
    w_qkv = qkv_all[:, :chip_rows].reshape(16 * chip_rows, QKV_HALF)
    small_all = qkv_all[:, chip_rows:].reshape(16, -1)[:, : small_rows * rows]
    small_all = small_all.reshape(16, small_rows, rows).astype(F32)
    w_rest = lax.all_gather(dense_half[:, QKV_HALF:], CHIPS, axis=0, tiled=True)
    w_o = w_rest[:, : HALF_WIDTHS[3]]
    at = HALF_WIDTHS[3]
    w_gu = w_rest[:, at : at + 2 * HALF_WIDTHS[4]]
    w_d = w_rest[:, at + 2 * HALF_WIDTHS[4] :]

    expert_own = lax.all_gather(expert_weights[0].astype(BF), DEPTH, axis=0, tiled=True)
    expert_other = swap(expert_own)
    experts = [
        jnp.where(first_core, expert_own, expert_other),
        jnp.where(first_core, expert_other, expert_own),
    ]

    places = jnp.arange(width, dtype=jnp.int32)
    source = jnp.repeat(chips, chip_rows) * chip_rows + places % chip_rows
    order = (places[:, None] == source[None, :]).astype(BF)

    inputs = tokens[0].astype(F32)
    h_one_f, normed_one, factor_one = norm_forward(inputs, gains[0])
    h_one = dot(of_chip(h_one_f.astype(BF)), order).astype(BF)
    upstream = cotangent[0]
    upstream_f = upstream.astype(F32)
    cot_all = lax.all_gather(upstream, CHIPS, axis=0, tiled=True).reshape(16, rows, width)
    cot_chip = of_chip(upstream)

    projected = dot(h_one, w_qkv)
    query = projected[:, : HALF_WIDTHS[0]].astype(BF)
    kv_all = gather_plane(projected[:, HALF_WIDTHS[0] :].astype(BF))

    segments_all = (small_all[:, :2] * 64.0 + small_all[:, 2:4]).reshape(-1)
    routes_all = small_all[:, 4 : 4 + TOP]
    high, mid_term, low_term = (
        small_all[:, 4 + k * TOP : 4 + (k + 1) * TOP] for k in range(1, 4)
    )
    gates_all = high + mid_term + low_term
    earlier = jnp.triu(jnp.ones((rows, rows), F32), 1).astype(BF)
    picks, gate_slots = [], []
    for local in range(2):
        named = routes_all == (chip * 2 + local).astype(F32)
        hit = jnp.any(named, axis=1)
        gate = jnp.sum(jnp.where(named, gates_all, 0.0), axis=1)
        slot = dot(hit.astype(BF), earlier).astype(jnp.int32)
        pick = hit[:, None, :] & (
            slot[:, None, :] == jnp.arange(cap, dtype=jnp.int32)[None, :, None]
        )
        picks.append(pick.astype(BF))
        gate_slots.append(jnp.sum(jnp.where(pick, gate[:, None, :], 0.0), axis=2, keepdims=True))
    pick = jnp.concatenate(picks, axis=1)
    gate_slot = jnp.concatenate(gate_slots, axis=1)
    ones = jnp.ones_like(gate_slot)

    query_spots = first_of_chip + jnp.arange(2 * rows, dtype=jnp.int32)
    run_start = jnp.sum(
        (segments_all[None, :] < segments_chip.reshape(-1, 1)).astype(jnp.int32), axis=1
    )
    query_range = jnp.concatenate(
        [run_start[None], query_spots[None], jnp.zeros((6, 2 * rows), jnp.int32)], axis=0
    )
    key_spots = (
        chips[:, None] * (2 * rows) + jnp.arange(2 * rows, dtype=jnp.int32)[None, :]
    ).reshape(-1, 1)
    attn_f, lse = attend(key_spots, query_range, query, kv_all, scale)
    attn = attn_f.astype(BF)
    resid = inputs + summed_for_own(times_transposed(attn, w_o))
    h_two_f, normed_two, factor_two = norm_forward(resid, gains[1])
    h_two = h_two_f.astype(BF)

    h_two_all = gather_plane(h_two).reshape(16, rows, width)
    h_two_chip = of_chip(h_two)
    x_both = pick_rows(jnp.arange(16, dtype=jnp.int32), pick, ones, h_two_all)
    d_out_both = pick_rows(chips, pick, gate_slot, cot_all)
    outs, d_xs, expert_grads = [], [], []
    for local in range(2):
        weights = experts[local]
        x = x_both[local].reshape(16 * cap, width)
        pre = dot(x, weights[:, : 2 * EXPERT_FF])
        gate_pre, up_pre = pre[:, :EXPERT_FF], pre[:, EXPERT_FF:]
        act, deriv = silu_parts(gate_pre)
        mid = (act * up_pre).astype(BF)
        outs.append(times_transposed(mid, weights[:, 2 * EXPERT_FF :]).astype(BF))
        d_out = d_out_both[local].reshape(16 * cap, width)
        d_mid = dot(d_out, weights[:, 2 * EXPERT_FF :])
        d_pre = jnp.concatenate(
            [(d_mid * up_pre * deriv).astype(BF), (d_mid * act).astype(BF)], axis=1
        )
        d_xs.append(times_transposed(d_pre, weights[:, : 2 * EXPERT_FF]).astype(BF))
        expert_grads.append(
            jnp.concatenate(
                [
                    row_major(transposed_times(x, d_pre).astype(BF)),
                    row_major(transposed_times(d_out, mid).astype(BF)),
                ],
                axis=1,
            )
        )
    d_x_both = jnp.stack(d_xs).reshape(2, 16, cap, width)
    grad_h_experts = sum_plane(unpick_rows(pick, ones, d_x_both))
    out_both = jnp.stack(outs).reshape(2, 16, cap, width)
    mixture = sum_plane(unpick_rows(pick, gate_slot, out_both))

    own_part = jnp.where(first_core, expert_grads[0], expert_grads[1])
    other_part = jnp.where(first_core, expert_grads[1], expert_grads[0])
    expert_local = row_major((own_part.astype(F32) + swap(other_part).astype(F32)).astype(BF))
    expert_grad = lax.psum_scatter(expert_local, DEPTH, scatter_dimension=0, tiled=True)
    expert_grad = row_major(expert_grad).astype(F32)

    shared_pre = dot(h_two_chip, w_gu)
    half_ff = HALF_WIDTHS[4]
    shared_gate, shared_up = shared_pre[:, :half_ff], shared_pre[:, half_ff:]
    shared_act, shared_deriv = silu_parts(shared_gate)
    shared_mid = (shared_act * shared_up).astype(BF)
    shared_out = summed_for_own(times_transposed(shared_mid, w_d))
    block_out = (resid + shared_out + mixture).astype(BF)
    grad_shared_mid = dot(cot_chip, w_d)
    grad_shared = jnp.concatenate(
        [
            (grad_shared_mid * shared_up * shared_deriv).astype(BF),
            (grad_shared_mid * shared_act).astype(BF),
        ],
        axis=1,
    )
    grad_h_two = summed_for_own(times_transposed(grad_shared, w_gu)) + grad_h_experts
    grad_resid_norm, gain_two_part = norm_backward(grad_h_two, normed_two, factor_two, gains[1])
    grad_resid = upstream_f + grad_resid_norm
    grad_att = of_chip(grad_resid.astype(BF))
    grad_attn = dot(grad_att, w_o).astype(BF)

    delta = jnp.sum(
        (grad_attn.astype(F32) * attn_f).reshape(2 * rows, HEADS_HALF, HEAD_DIM), axis=2
    ).T
    delta = jnp.pad(delta, ((0, 8 - HEADS_HALF), (0, 0)))
    grad_query, kv_terms = attend_back(
        key_spots, query_range, query, grad_attn, lse, delta, kv_all, scale
    )
    grad_kv = sum_plane(kv_terms).astype(BF)
    grad_qkv = jnp.concatenate([grad_query, grad_kv], axis=1)
    grad_h_one = times_transposed(grad_qkv, w_qkv).astype(BF)
    grad_h_one = summed_for_own(times_transposed(grad_h_one, order).astype(BF).astype(F32))
    grad_input_norm, gain_one_part = norm_backward(grad_h_one, normed_one, factor_one, gains[0])
    input_grad = grad_resid + grad_input_norm

    grads_rest = jnp.concatenate(
        [
            row_major(transposed_times(grad_att, attn).astype(BF)),
            row_major(transposed_times(h_two_chip, grad_shared).astype(BF)),
            row_major(transposed_times(cot_chip, shared_mid).astype(BF)),
        ],
        axis=1,
    )
    rest_sum = lax.psum_scatter(grads_rest, CHIPS, scatter_dimension=0, tiled=True)
    qkv_sum = sum_plane(transposed_times(h_one, grad_qkv).astype(BF))
    half_sum = jnp.concatenate([qkv_sum.astype(BF), rest_sum], axis=1)
    blocks = lax.all_to_all(
        half_sum.reshape(8, chip_rows // 8, HALF_COLS), COLUMN, 0, 0, tiled=True
    )
    blocks = jnp.sum(blocks.reshape(2, 4, chip_rows // 8, HALF_COLS).astype(F32), axis=1)
    dense_grad = whole_of(blocks[0], blocks[1])

    gain_part = jnp.stack([gain_one_part, gain_two_part])
    local_squares = jnp.sum(dense_grad * dense_grad) + jnp.sum(expert_grad * expert_grad)
    gain_tiles = gain_part.size // 128
    packed = jnp.concatenate(
        [
            gain_part.reshape(gain_tiles, 128),
            jnp.broadcast_to(local_squares, (8, 128)),
        ],
        axis=0,
    )
    packed = total_over_all(packed)
    gain_grad = packed[:gain_tiles].reshape(gain_part.shape)
    total_squares = packed[gain_tiles, 0]
    grad_norm = jnp.sqrt(total_squares + jnp.sum(gain_grad * gain_grad))
    clip_factor = jnp.minimum(1.0, CLIP_NORM / (grad_norm + 1e-06))
    dense_new, dense_first_new, dense_second_new = adamw_step(
        dense_weights,
        dense_first,
        dense_second,
        dense_grad * clip_factor,
        MATRIX_RATE,
        WEIGHT_DECAY,
    )
    expert_new, expert_first_new, expert_second_new = adamw_step(
        expert_weights,
        expert_first,
        expert_second,
        expert_grad[None] * clip_factor,
        MATRIX_RATE,
        WEIGHT_DECAY,
    )
    gain_cols = gain_first.shape[1]
    gain_begin = lax.axis_index(ALL) * gain_cols
    gain_slice = lax.dynamic_slice_in_dim(gains, gain_begin, gain_cols, 1)
    gain_grad_slice = lax.dynamic_slice_in_dim(gain_grad, gain_begin, gain_cols, 1)
    gain_new, gain_first_new, gain_second_new = adamw_step(
        gain_slice, gain_first, gain_second, gain_grad_slice * clip_factor, GAIN_RATE, 0.0
    )
    return (
        block_out[None],
        input_grad[None],
        grad_norm,
        dense_new,
        dense_first_new,
        dense_second_new,
        expert_new,
        expert_first_new,
        expert_second_new,
        gain_new,
        gain_first_new,
        gain_second_new,
    )


def solution(mesh):
    fine = Mesh(mesh.devices.reshape(4, 4, 2, 2, 2), ALL)
    sequence = (DEPTH, CTX)
    token = P(*sequence, None)
    dense = P(ALL, None)
    expert = P(CTX, DEPTH, None)
    gain = P(None, ALL)
    return jax.shard_map(
        shards,
        mesh=fine,
        in_specs=(
            token,
            token,
            P(*sequence),
            token,
            token,
            dense,
            dense,
            dense,
            expert,
            expert,
            expert,
            P(),
            gain,
            gain,
        ),
        out_specs=(
            token,
            token,
            P(),
            dense,
            dense,
            dense,
            expert,
            expert,
            expert,
            gain,
            gain,
            gain,
        ),
        check_vma=False,
    )
```

```python
import functools

import jax
import jax.numpy as jnp
from jax import lax
from jax.experimental import pallas as pl
from jax.experimental.layout import Layout, with_layout_constraint
from jax.experimental.pallas import tpu as pltpu
from jax.sharding import Mesh
from jax.sharding import PartitionSpec as P

HEADS = 12
KV_HEADS = 4
HEAD_DIM = 128
GROUP = HEADS // KV_HEADS
EXPERT_FF = 512
SHARED_FF = 1024
TOP = 6
STEP = 10

EPS_NORM = 1e-05
CLIP_NORM = 1.0
FIRST_DECAY = 0.9
SECOND_DECAY = 0.95
ADAM_EPS = 1e-08
WEIGHT_DECAY = 0.1
MATRIX_RATE = 0.05
GAIN_RATE = 0.6
NEGATIVE = -1e30

QW = HEADS * HEAD_DIM
KW = KV_HEADS * HEAD_DIM
STARTS = (0, QW, QW + KW, QW + 2 * KW, 2 * QW + 2 * KW, 2 * QW + 2 * KW + SHARED_FF, 2 * QW + 2 * KW + 2 * SHARED_FF)
WIDTHS = (QW, KW, KW, QW, SHARED_FF, SHARED_FF, SHARED_FF)
HALF_WIDTHS = tuple(w // 2 for w in WIDTHS)
HALF_COLS = sum(HALF_WIDTHS)
QKV_HALF = sum(HALF_WIDTHS[:3])
QKVO_HALF = sum(HALF_WIDTHS[:4])
SHARED_PART = SHARED_FF // 8
MINE = QKVO_HALF + 3 * SHARED_PART
HEADS_HALF = HEADS // 2
KV_HALF = KV_HEADS // 2

CHIPS = ("y", "x")
CTX = ("y", "x", "core")
DEPTH = ("wt", "seq")
COLUMN = ("core", "wt", "seq")
ALL = CTX + DEPTH
BF = jnp.bfloat16
F32 = jnp.float32
LOG2E = 1.4426950408889634
MIB = 1 << 20
CHUNK = 512


def turn(v, phase, step):
    pairs = []
    for y in range(4):
        for x in range(4):
            for core in range(2):
                along_x = (phase == 1) == (core == 0)
                ty, tx = (y, (x + step) % 4) if along_x else ((y + step) % 4, x)
                pairs.append(((y * 4 + x) * 2 + core, (ty * 4 + tx) * 2 + core))
    return lax.ppermute(v, CTX, pairs)


def swap(v):
    return lax.ppermute(v, "core", [(0, 1), (1, 0)])


def ring_pieces(v, phase):
    return [v, turn(v, phase, 1), turn(v, phase, -1), turn(v, phase, 2)]


def gather_plane(v, wait=None):
    v = jnp.concatenate(ring_pieces(v, 1), axis=0)
    return ring_pieces(v if wait is None else v + wait.astype(v.dtype), 2)


def ring_sum(pieces, phase):
    own, left, right, far = pieces
    terms = [own, turn(left, phase, -1), turn(right, phase, 1), turn(far, phase, 2)]
    return sum(t.astype(F32) for t in terms)


def sum_plane(pieces, wait=0.0):
    g = (ring_sum(pieces, 2) + wait).astype(BF)
    rows = g.shape[0] // 4
    return ring_sum([g[k * rows : (k + 1) * rows] for k in range(4)], 1)


def zero_after(v):
    return jnp.minimum(jnp.abs(v[(0,) * v.ndim].astype(F32)), 0.0)


def block_chips(iy, ix, first_core):
    offsets = jnp.array([0, 3, 1, 2], jnp.int32)
    outer, inner = jnp.repeat(offsets, 4), jnp.tile(offsets, 4)
    y = (iy + jnp.where(first_core, outer, inner)) % 4
    x = (ix + jnp.where(first_core, inner, outer)) % 4
    return y * 4 + x


def row_major(v):
    return with_layout_constraint(v, Layout(tuple(range(v.ndim))))


def pieces_of(refs, rows):
    return [(refs[b // 4], b % 4 * rows) for b in range(16)]


def spread_kernel(dense, out):
    for core in range(2):
        for z in range(4):
            at = 0
            for k, (start, width) in enumerate(zip(STARTS, HALF_WIDTHS, strict=True)):
                first = start + core * width
                if k >= 4:
                    width //= 4
                    first += z * width
                out[core * 4 + z, :, at : at + width] = dense[:, first : first + width].astype(BF)
                at += width


def spread(dense):
    return pl.pallas_call(
        spread_kernel,
        out_shape=jax.ShapeDtypeStruct((8, dense.shape[0], MINE), BF),
        compiler_params=pltpu.CompilerParams(vmem_limit_bytes=8 * MIB),
    )(dense)


def project_kernel(chips, h, p0, p1, p2, p3, query, kv, weights, small, held, small_held, sems, out_sem):
    extra = small_held.shape[0] // 16
    rows = p0.shape[0] // 4 - extra
    needed, others = [], []
    for b, (ref, row) in enumerate(pieces_of((p0, p1, p2, p3), rows + extra)):
        to = pl.ds(pl.multiple_of(chips[b] * rows, rows), rows)
        needed.append(
            pltpu.make_async_copy(ref.at[pl.ds(row, rows), :], held.at[to, :], sems.at[b, 0])
        )
        others.append(
            pltpu.make_async_copy(
                ref.at[pl.ds(row + rows, extra), :],
                small_held.at[pl.ds(b * extra, extra), :],
                sems.at[b, 1],
            )
        )
    for copy in needed + others:
        copy.start()
    for copy in needed:
        copy.wait()
    out = pltpu.make_async_copy(held, weights, out_sem.at[0])
    out.start()
    split = query.shape[1]
    query[...] = dot(h[...], held[:, :split]).astype(BF)
    kv[...] = dot(h[...], held[:, split : split + kv.shape[1]]).astype(BF)
    for b, copy in enumerate(others):
        copy.wait()
        small[b] = small_held[b * extra : b * extra + 8, :].astype(F32)
    out.wait()


def project(chips, h, pieces, extra):
    rows, width = h.shape
    cols = pieces[0].shape[1]
    anywhere, vectors = pl.BlockSpec(memory_space=pl.ANY), pl.BlockSpec(memory_space=pltpu.VMEM)
    return pl.pallas_call(
        project_kernel,
        in_specs=[pl.BlockSpec(memory_space=pltpu.SMEM), vectors] + [anywhere] * 4,
        out_specs=[vectors, vectors, anywhere, vectors],
        out_shape=[
            jax.ShapeDtypeStruct((rows, HALF_WIDTHS[0]), BF),
            jax.ShapeDtypeStruct((rows, QKV_HALF - HALF_WIDTHS[0]), BF),
            jax.ShapeDtypeStruct((width, cols), BF),
            jax.ShapeDtypeStruct((16, 8, cols), F32),
        ],
        scratch_shapes=[
            pltpu.VMEM((width, cols), BF),
            pltpu.VMEM((16 * extra, cols), BF),
            pltpu.SemaphoreType.DMA((16, 2)),
            pltpu.SemaphoreType.DMA((1,)),
        ],
        cost_estimate=pl.CostEstimate(
            flops=2 * rows * width * QKV_HALF, bytes_accessed=16 * MIB, transcendentals=0
        ),
        compiler_params=pltpu.CompilerParams(vmem_limit_bytes=18 * MIB),
    )(chips, h, *pieces)


def shared_kernel(h_ref, up_ref, w_ref, out_ref, dh_ref, grad_ref):
    @pl.when(pl.program_id(0) == 0)
    def _():
        out_ref[...] = jnp.zeros_like(out_ref)
        dh_ref[...] = jnp.zeros_like(dh_ref)

    h, upstream = h_ref[...], up_ref[...]
    w_gu, w_d = w_ref[:, : 2 * SHARED_PART], w_ref[:, 2 * SHARED_PART :]
    pre = dot(h, w_gu)
    gate, up = pre[:, :SHARED_PART], pre[:, SHARED_PART:]
    act, deriv = silu_parts(gate)
    mid = (act * up).astype(BF)
    d_mid = dot(upstream, w_d)
    d_pre = jnp.concatenate([(d_mid * up * deriv).astype(BF), (d_mid * act).astype(BF)], axis=1)
    out_ref[...] += times_transposed(mid, w_d)
    dh_ref[...] += times_transposed(d_pre, w_gu)
    grad_ref[:, : 2 * SHARED_PART] = transposed_times(h, d_pre).astype(BF)
    grad_ref[:, 2 * SHARED_PART :] = transposed_times(upstream, mid).astype(BF)


def shared_expert(h, upstream, weights):
    rows, width = h.shape
    cols = weights.shape[1]
    whole = pl.BlockSpec((rows, width), lambda z: (0, 0))
    part = pl.BlockSpec((width, cols), lambda z: (z, 0))
    return pl.pallas_call(
        shared_kernel,
        grid=(4,),
        in_specs=[whole, whole, part],
        out_specs=[whole, whole, part],
        out_shape=[
            jax.ShapeDtypeStruct((rows, width), F32),
            jax.ShapeDtypeStruct((rows, width), F32),
            jax.ShapeDtypeStruct(weights.shape, BF),
        ],
        cost_estimate=pl.CostEstimate(
            flops=6 * rows * width * cols * 4, bytes_accessed=14 * MIB, transcendentals=rows * 512
        ),
        compiler_params=pltpu.CompilerParams(vmem_limit_bytes=18 * MIB),
    )(h, upstream, weights)


def by_visibility(bounds, first, second, length, run):
    start_low, start_high, low, high = (bounds[k] for k in range(4))
    last = length - 1

    def whole(at):
        return (at >= start_high) & (at + last <= low)

    def some(at):
        return (at + last >= start_low) & (at <= high)

    all_seen = whole(first) & whole(second)
    any_seen = some(first) | some(second)
    pl.when(all_seen)(lambda: run(False))
    pl.when(any_seen & jnp.logical_not(all_seen))(lambda: run(True))


def seen(query_range, first, second, length):
    spots = lax.broadcasted_iota(jnp.int32, (length, query_range.shape[1]), 0)
    parts = []
    for at in (first, second):
        parts.append(
            (spots >= query_range[0:1, :] - at) & (spots <= query_range[1:2, :] - at)
        )
    return parts


def attend_kernel(scale, chips, bounds, ranges, q_ref, p0, p1, p2, p3, out_ref, lse_ref, acc, top, total):
    acc[...] = jnp.zeros_like(acc)
    total[...] = jnp.zeros_like(total)
    top[...] = jnp.full_like(top, -jnp.inf)
    rows = q_ref.shape[0]
    places = pieces_of((p0, p1, p2, p3), rows)
    for b in range(0, 16, 2):
        ref, row = places[b]
        block = pl.ds(row, 2 * rows)
        first, second = chips[b] * rows, chips[b + 1] * rows

        def run(masked, ref=ref, block=block, first=first, second=second):
            if masked:
                visible = jnp.concatenate(seen(ranges[...], first, second, rows), axis=0)
            for head in range(HEADS_HALF):
                kv_head = head // GROUP
                cols = slice(head * HEAD_DIM, (head + 1) * HEAD_DIM)
                k_at, v_at = kv_head * HEAD_DIM, (KV_HALF + kv_head) * HEAD_DIM
                key = ref[block, k_at : k_at + HEAD_DIM]
                value = ref[block, v_at : v_at + HEAD_DIM]
                scores = times_transposed(key, q_ref[:, cols]) * (scale * LOG2E)
                if masked:
                    scores = jnp.where(visible, scores, NEGATIVE)
                before = top[head : head + 1, :]
                now = jnp.maximum(before, jnp.max(scores, axis=0, keepdims=True))
                expo = jnp.exp2(scores - now)
                fade = jnp.exp2(before - now)
                top[head : head + 1, :] = now
                total[head : head + 1, :] = total[head : head + 1, :] * fade + jnp.sum(
                    expo, axis=0, keepdims=True
                )
                acc[cols, :] = acc[cols, :] * fade + transposed_times(value, expo.astype(BF))

        by_visibility(bounds, first, second, rows, run)
    for head in range(HEADS_HALF):
        cols = slice(head * HEAD_DIM, (head + 1) * HEAD_DIM)
        out_ref[:, cols] = (acc[cols, :] / total[head : head + 1, :]).T
    lse_ref[...] = top[...] + jnp.log2(total[...])


def attend(chips, bounds, ranges, query, pieces, scale):
    rows, cols = query.shape
    keys = 16 * rows
    in_scalars, in_vectors = pl.BlockSpec(memory_space=pltpu.SMEM), pl.BlockSpec(memory_space=pltpu.VMEM)
    return pl.pallas_call(
        functools.partial(attend_kernel, scale),
        in_specs=[in_scalars] * 2 + [in_vectors] * 6,
        out_specs=[in_vectors] * 2,
        out_shape=[
            jax.ShapeDtypeStruct((rows, cols), F32),
            jax.ShapeDtypeStruct((8, rows), F32),
        ],
        scratch_shapes=[
            pltpu.VMEM((cols, rows), F32),
            pltpu.VMEM((8, rows), F32),
            pltpu.VMEM((8, rows), F32),
        ],
        cost_estimate=pl.CostEstimate(
            flops=4 * rows * cols * keys, bytes_accessed=8 * MIB, transcendentals=rows * keys * 6
        ),
        compiler_params=pltpu.CompilerParams(vmem_limit_bytes=18 * MIB),
    )(chips, bounds, ranges, query, *pieces)


def attend_back_kernel(
    scale, chips, bounds, ranges, q_ref, do_ref, o_ref, lse_ref, p0, p1, p2, p3,
    dq_ref, g0, g1, g2, g3, acc, delta
):
    acc[...] = jnp.zeros_like(acc)
    for head in range(HEADS_HALF):
        cols = slice(head * HEAD_DIM, (head + 1) * HEAD_DIM)
        shared = do_ref[:, cols].astype(F32) * o_ref[:, cols]
        delta[head : head + 1, :] = jnp.sum(shared.T, axis=0, keepdims=True)
    rows = q_ref.shape[0]
    places = pieces_of((p0, p1, p2, p3), rows)
    grads = pieces_of((g0, g1, g2, g3), rows)
    for b in range(0, 16, 2):
        ref, row = places[b]
        out = grads[b][0]
        block = pl.ds(row, 2 * rows)
        first, second = chips[b] * rows, chips[b + 1] * rows
        out[block, :] = jnp.zeros((2 * rows, out.shape[1]), BF)

        def run(masked, ref=ref, out=out, block=block, first=first, second=second):
            if masked:
                visible = jnp.concatenate(seen(ranges[...], first, second, rows), axis=0)
            for kv_head in range(KV_HALF):
                k_at, v_at = kv_head * HEAD_DIM, (KV_HALF + kv_head) * HEAD_DIM
                key = ref[block, k_at : k_at + HEAD_DIM]
                value = ref[block, v_at : v_at + HEAD_DIM]
                key_grad = jnp.zeros(key.shape, F32)
                value_grad = jnp.zeros(key.shape, F32)
                for member in range(GROUP):
                    head = kv_head * GROUP + member
                    cols = slice(head * HEAD_DIM, (head + 1) * HEAD_DIM)
                    query, upstream = q_ref[:, cols], do_ref[:, cols]
                    scores = times_transposed(key, query) * (scale * LOG2E)
                    if masked:
                        scores = jnp.where(visible, scores, NEGATIVE)
                    chances = jnp.exp2(scores - lse_ref[head : head + 1, :])
                    inner = times_transposed(value, upstream)
                    grad_scores = (chances * (inner - delta[head : head + 1, :])).astype(BF)
                    value_grad += dot(chances.astype(BF), upstream)
                    key_grad += dot(grad_scores, query)
                    acc[cols, :] += transposed_times(key, grad_scores)
                out[block, k_at : k_at + HEAD_DIM] = (key_grad * scale).astype(BF)
                out[block, v_at : v_at + HEAD_DIM] = value_grad.astype(BF)

        by_visibility(bounds, first, second, rows, run)
    for head in range(HEADS_HALF):
        cols = slice(head * HEAD_DIM, (head + 1) * HEAD_DIM)
        dq_ref[:, cols] = (acc[cols, :] * scale).T.astype(BF)


def attend_back(chips, bounds, ranges, query, upstream, out_f, lse, pieces, scale):
    rows, cols = query.shape
    keys = 16 * rows
    in_scalars, in_vectors = pl.BlockSpec(memory_space=pltpu.SMEM), pl.BlockSpec(memory_space=pltpu.VMEM)
    return pl.pallas_call(
        functools.partial(attend_back_kernel, scale),
        in_specs=[in_scalars] * 2 + [in_vectors] * 9,
        out_specs=[in_vectors] * 5,
        out_shape=[jax.ShapeDtypeStruct((rows, cols), BF)]
        + [jax.ShapeDtypeStruct(p.shape, BF) for p in pieces],
        scratch_shapes=[pltpu.VMEM((cols, rows), F32), pltpu.VMEM((8, rows), F32)],
        cost_estimate=pl.CostEstimate(
            flops=10 * rows * cols * keys, bytes_accessed=12 * MIB, transcendentals=rows * keys * 6
        ),
        compiler_params=pltpu.CompilerParams(vmem_limit_bytes=24 * MIB),
    )(chips, bounds, ranges, query, upstream, out_f, lse, *pieces)


def pick_kernel(order, pick, scale, *refs):
    sources, (out, held, ready, in_sems, out_sems) = refs[:4], refs[4:]
    pairs, slots, rows = pick.shape
    half, width = slots // 2, held.shape[1]
    copies = [
        pltpu.make_async_copy(
            sources[p // 2].at[pl.ds(p % 2 * rows, rows), :],
            held.at[pl.ds(p * rows, rows), :],
            in_sems.at[p],
        )
        for p in range(pairs)
    ]
    for copy in copies:
        copy.start()
    sent = []
    for p in range(pairs):
        copies[p].wait()
        for at in range(0, width, CHUNK):
            cols = slice(at, at + CHUNK)
            found = dot(pick[p], held[pl.ds(p * rows, rows), cols])
            if scale is not None:
                found = found * scale[p]
            found = found.astype(BF)
            for e in range(2):
                ready[e, pl.ds(p * half, half), cols] = found[e * half : (e + 1) * half]
        for e in range(2):
            to = pl.ds(p * half, half)
            sent.append(
                pltpu.make_async_copy(ready.at[e, to, :], out.at[e, to, :], out_sems.at[p, e])
            )
            sent[-1].start()
    for copy in sent:
        copy.wait()


def pick_rows(order, pick, scale, sources):
    pairs, slots, rows = pick.shape
    width = sources[0].shape[1]
    vectors, anywhere = pl.BlockSpec(memory_space=pltpu.VMEM), pl.BlockSpec(memory_space=pl.ANY)
    given = [pick] if scale is None else [pick, scale]

    def kernel(order_ref, pick_ref, *refs):
        if scale is None:
            pick_kernel(order_ref, pick_ref, None, *refs)
        else:
            pick_kernel(order_ref, pick_ref, *refs)

    return pl.pallas_call(
        kernel,
        in_specs=[pl.BlockSpec(memory_space=pltpu.SMEM)]
        + [vectors] * len(given)
        + [anywhere] * 4,
        out_specs=anywhere,
        out_shape=jax.ShapeDtypeStruct((2, pairs * slots // 2, width), BF),
        scratch_shapes=[
            pltpu.VMEM((pairs * rows, width), BF),
            pltpu.VMEM((2, pairs * slots // 2, width), BF),
            pltpu.SemaphoreType.DMA((pairs,)),
            pltpu.SemaphoreType.DMA((pairs, 2)),
        ],
        cost_estimate=pl.CostEstimate(
            flops=2 * pairs * slots * rows * width, bytes_accessed=12 * MIB, transcendentals=0
        ),
        compiler_params=pltpu.CompilerParams(vmem_limit_bytes=18 * MIB),
    )(order, *given, *sources)


def unpick_kernel(pick, scale, own, other, o0, o1, o2, o3, held, ready, in_sems, out_sems):
    pairs, slots, rows = pick.shape
    half, width = slots // 2, held.shape[1]
    outs = (o0, o1, o2, o3)
    copies = []
    for p in range(pairs):
        for e, ref in enumerate((own, other)):
            copies.append(
                pltpu.make_async_copy(
                    ref.at[pl.ds(p * half, half), :],
                    held.at[pl.ds(p * slots + e * half, half), :],
                    in_sems.at[p, e],
                )
            )
            copies[-1].start()
    sent = []
    for p in range(pairs):
        copies[2 * p].wait()
        copies[2 * p + 1].wait()
        to = pl.ds(p * rows, rows)
        for at in range(0, width, CHUNK):
            cols = slice(at, at + CHUNK)
            given = held[pl.ds(p * slots, slots), cols]
            if scale is not None:
                given = (given.astype(F32) * scale[p]).astype(BF)
            ready[to, cols] = transposed_times(pick[p], given).astype(BF)
        sent.append(
            pltpu.make_async_copy(
                ready.at[to, :], outs[p // 2].at[pl.ds(p % 2 * rows, rows), :], out_sems.at[p]
            )
        )
        sent[-1].start()
    for copy in sent:
        copy.wait()


def unpick_rows(pick, scale, own, other):
    pairs, slots, rows = pick.shape
    width = own.shape[1]
    vectors, anywhere = pl.BlockSpec(memory_space=pltpu.VMEM), pl.BlockSpec(memory_space=pl.ANY)
    given = [pick] if scale is None else [pick, scale]

    def kernel(pick_ref, *refs):
        if scale is None:
            unpick_kernel(pick_ref, None, *refs)
        else:
            unpick_kernel(pick_ref, *refs)

    return pl.pallas_call(
        kernel,
        in_specs=[vectors] * len(given) + [anywhere] * 2,
        out_specs=[anywhere] * 4,
        out_shape=[jax.ShapeDtypeStruct((pairs * rows // 4, width), BF)] * 4,
        scratch_shapes=[
            pltpu.VMEM((pairs * slots, width), BF),
            pltpu.VMEM((pairs * rows, width), BF),
            pltpu.SemaphoreType.DMA((pairs, 2)),
            pltpu.SemaphoreType.DMA((pairs,)),
        ],
        cost_estimate=pl.CostEstimate(
            flops=2 * pairs * slots * rows * width, bytes_accessed=12 * MIB, transcendentals=0
        ),
        compiler_params=pltpu.CompilerParams(vmem_limit_bytes=18 * MIB),
    )(*given, own, other)


def total_over_all(v):
    v = v + swap(v)
    for axis in ("x", "y"):
        v = v + lax.ppermute(v, axis, [(i, i ^ 1) for i in range(4)])
        v = v + lax.ppermute(v, axis, [(i, i ^ 3) for i in range(4)])
    for axis in DEPTH:
        v = v + lax.ppermute(v, axis, [(0, 1), (1, 0)])
    return v


def silu_parts(values):
    sigmoid_values = jax.nn.sigmoid(values)
    return (values * sigmoid_values, sigmoid_values * (1.0 + values * (1.0 - sigmoid_values)))


def norm_forward(values, gain_row):
    factor = lax.rsqrt(jnp.mean(values * values, axis=-1, keepdims=True) + EPS_NORM)
    normed = values * factor
    return (normed * gain_row, normed, factor)


def norm_backward(upstream, normed, factor, gain_row):
    scaled = upstream * gain_row
    inward = factor * (scaled - normed * jnp.mean(scaled * normed, axis=-1, keepdims=True))
    return (inward, jnp.sum(upstream * normed, axis=0))


def adamw_step(weight, first_moment, second, gradient, step_rate, decay_rate):
    first_moment = FIRST_DECAY * first_moment + (1.0 - FIRST_DECAY) * gradient
    second = SECOND_DECAY * second + (1.0 - SECOND_DECAY) * gradient * gradient
    first_hat = first_moment / (1.0 - FIRST_DECAY**STEP)
    second_hat = second / (1.0 - SECOND_DECAY**STEP)
    weight = weight - step_rate * (
        first_hat / (jnp.sqrt(second_hat) + ADAM_EPS) + decay_rate * weight
    )
    return (weight, first_moment, second)


def dot(left, right):
    return jnp.dot(left, right, preferred_element_type=F32)


def times_transposed(left, right):
    return lax.dot_general(left, right, (((1,), (1,)), ((), ())), preferred_element_type=F32)


def transposed_times(left, right):
    return lax.dot_general(left, right, (((0,), (0,)), ((), ())), preferred_element_type=F32)


def whole_of(halves, quarters):
    columns, at = [], 0
    for width in HALF_WIDTHS[:4]:
        columns += [halves[core][:, at : at + width] for core in range(2)]
        at += width
    part = HALF_WIDTHS[4] // 4
    for k in range(3):
        columns += [
            quarters[core, z][:, k * part : (k + 1) * part] for core in range(2) for z in range(4)
        ]
    return jnp.concatenate(columns, axis=1)


def shards(
    tokens,
    cotangent,
    segment_ids,
    routes,
    gates,
    dense_weights,
    dense_first,
    dense_second,
    expert_weights,
    expert_first,
    expert_second,
    gains,
    gain_first,
    gain_second,
):
    rows = tokens.shape[1]
    width = tokens.shape[2]
    seq_len = rows * 32
    cap = min(rows, 2 * rows * TOP // 32)
    scale = HEAD_DIM ** (-0.5)
    iy, ix, core = lax.axis_index("y"), lax.axis_index("x"), lax.axis_index("core")
    chip = iy * 4 + ix
    first_core = core == 0
    first_of_chip = chip * 2 * rows

    def both_cores(mine, other):
        return jnp.where(
            first_core,
            jnp.concatenate([mine, other], axis=0),
            jnp.concatenate([other, mine], axis=0),
        )

    def of_chip(v):
        return both_cores(v, swap(v))

    def own_rows(v):
        return lax.dynamic_slice_in_dim(v, core * rows, rows, 0)

    def other_rows(v):
        return lax.dynamic_slice_in_dim(v, (1 - core) * rows, rows, 0)

    def summed_for_own(v):
        return own_rows(v) + swap(other_rows(v))

    def three_terms(v):
        high = v.astype(BF)
        rest = v - high.astype(F32)
        mid = rest.astype(BF)
        return [high, mid, (rest - mid.astype(F32)).astype(BF)]

    segments_chip = of_chip(segment_ids[0][None].astype(F32)).reshape(1, 2 * rows)
    digits = jnp.concatenate(
        [jnp.floor(segments_chip / 64.0), segments_chip - 64.0 * jnp.floor(segments_chip / 64.0)],
        axis=0,
    ).astype(BF)
    small = jnp.concatenate(
        [digits.reshape(4, rows), routes[0].T.astype(BF), *three_terms(gates[0].T)], axis=0
    )
    small_rows = small.shape[0]
    extra = 16
    small = jnp.pad(small.reshape(-1), (0, extra * QKVO_HALF - small.size))
    small = small.reshape(extra, QKVO_HALF)

    chip_rows = 8 * dense_weights.shape[0]
    dense_part = lax.all_to_all(spread(dense_weights), COLUMN, 0, 0, tiled=True)
    dense_part = dense_part.reshape(chip_rows, MINE)
    chips = block_chips(iy, ix, first_core)
    qkvo = gather_plane(jnp.concatenate([dense_part[:, :QKVO_HALF], small], axis=0))

    inputs = tokens[0].astype(F32)
    h_one_f, normed_one, factor_one = norm_forward(inputs, gains[0])
    h_one = of_chip(h_one_f.astype(BF))
    upstream = cotangent[0]
    upstream_f = upstream.astype(F32)
    cot_chip = of_chip(upstream)

    expert_low = expert_weights[0].astype(BF)
    expert_own = lax.all_gather(expert_low, DEPTH, axis=0, tiled=True)
    experts = [expert_own, swap(expert_own)]

    query, kv_own, w_qkvo, small_all = project(chips, h_one, qkvo, extra)
    w_qkv, w_o = w_qkvo[:, :QKV_HALF], w_qkvo[:, QKV_HALF:]
    kv_all = gather_plane(kv_own)
    cot_all = gather_plane(upstream, zero_after(kv_all[3]))
    small_all = small_all.reshape(16, -1)[:, : small_rows * rows].reshape(16, small_rows, rows)

    shared_in = dense_part[:, QKVO_HALF:] + zero_after(expert_own).astype(BF)
    shared_quarter = lax.all_gather(shared_in, CHIPS, axis=0, tiled=True)
    shared_all = lax.all_gather(shared_quarter, DEPTH, axis=0, tiled=True)

    places = jnp.arange(width, dtype=jnp.int32)
    source = jnp.repeat(chips, chip_rows) * chip_rows + places % chip_rows
    order = (places[:, None] == source[None, :]).astype(BF)
    h_one_turned = dot(h_one, order).astype(BF)

    segments_all = (small_all[:, :2] * 64.0 + small_all[:, 2:4]).reshape(-1)
    routes_all = small_all[:, 4 : 4 + TOP]
    high, mid_term, low_term = (
        small_all[:, 4 + k * TOP : 4 + (k + 1) * TOP] for k in range(1, 4)
    )
    gates_all = high + mid_term + low_term
    earlier = jnp.triu(jnp.ones((rows, rows), F32), 1).astype(BF)
    picks, gate_slots = [], []
    for local in range(2):
        expert_at = chip * 2 + (core if local == 0 else 1 - core)
        named = routes_all == expert_at.astype(F32)
        hit = jnp.any(named, axis=1)
        gate = jnp.sum(jnp.where(named, gates_all, 0.0), axis=1)
        slot = dot(hit.astype(BF), earlier).astype(jnp.int32)
        slot = (slot.reshape(8, 2, rows) + jnp.array([0, cap], jnp.int32)[:, None]).reshape(8, -1)
        hit, gate = hit.reshape(8, 2 * rows), gate.reshape(8, 2 * rows)
        pick = hit[:, None, :] & (
            slot[:, None, :] == jnp.arange(2 * cap, dtype=jnp.int32)[None, :, None]
        )
        picks.append(pick.astype(BF))
        gate_slots.append(jnp.sum(jnp.where(pick, gate[:, None, :], 0.0), axis=2, keepdims=True))
    pick = jnp.concatenate(picks, axis=1)
    gate_slot = jnp.concatenate(gate_slots, axis=1)

    query_spots = first_of_chip + jnp.arange(2 * rows, dtype=jnp.int32)
    run_start = jnp.sum(
        (segments_all[None, :] < segments_chip.reshape(-1, 1)).astype(jnp.int32), axis=1
    )
    ranges = jnp.concatenate(
        [run_start[None], query_spots[None], jnp.zeros((6, 2 * rows), jnp.int32)], axis=0
    )
    bounds = jnp.stack([run_start[0], run_start[-1], query_spots[0], query_spots[-1]])
    attn_f, lse = attend(chips, bounds, ranges, query, kv_all, scale)
    attn = (attn_f + (zero_after(cot_all[1]) + zero_after(cot_all[2]))).astype(BF)
    resid = inputs + summed_for_own(times_transposed(attn, w_o))
    h_two_f, normed_two, factor_two = norm_forward(resid, gains[1])
    h_two = h_two_f.astype(BF)

    h_two_all = gather_plane(h_two)
    h_two_chip = of_chip(h_two)
    shared_out, grad_h_shared, shared_grads = shared_expert(h_two_chip, cot_chip, shared_all)
    shared_grads = lax.psum_scatter(shared_grads, DEPTH, scatter_dimension=0, tiled=True)
    d_out_both = pick_rows(chips, pick, gate_slot, cot_all)
    later = (zero_after(shared_out) + zero_after(d_out_both)).astype(jnp.int32)
    x_both = pick_rows(chips + later, pick, None, h_two_all)
    outs, d_xs, expert_grads, down_grads = [], [], [], []
    for local in range(2):
        weights = experts[local]
        x = x_both[local]
        pre = dot(x, weights[:, : 2 * EXPERT_FF])
        gate_pre, up_pre = pre[:, :EXPERT_FF], pre[:, EXPERT_FF:]
        act, deriv = silu_parts(gate_pre)
        mid = (act * up_pre).astype(BF)
        outs.append(times_transposed(mid, weights[:, 2 * EXPERT_FF :]).astype(BF))
        d_out = d_out_both[local]
        d_mid = dot(d_out, weights[:, 2 * EXPERT_FF :])
        d_pre = jnp.concatenate(
            [(d_mid * up_pre * deriv).astype(BF), (d_mid * act).astype(BF)], axis=1
        )
        d_xs.append(times_transposed(d_pre, weights[:, : 2 * EXPERT_FF]).astype(BF))
        expert_grads.append(row_major(transposed_times(x, d_pre).astype(BF)))
        down_grads.append(row_major(transposed_times(d_out, mid).astype(BF)))
    expert_done = sum(zero_after(g) for g in expert_grads + down_grads)
    expert_grads = [
        jnp.concatenate(pair, axis=1) for pair in zip(expert_grads, down_grads, strict=True)
    ]
    grad_h_experts = sum_plane(unpick_rows(pick, None, *d_xs), expert_done)

    expert_local = (expert_grads[0].astype(F32) + swap(expert_grads[1]).astype(F32)).astype(BF)
    expert_grad = lax.psum_scatter(
        row_major(expert_local), DEPTH, scatter_dimension=0, tiled=True
    )
    expert_grad = row_major(expert_grad).astype(F32)

    shared_out = summed_for_own(shared_out)
    grad_h_two = summed_for_own(grad_h_shared) + grad_h_experts
    grad_resid_norm, gain_two_part = norm_backward(grad_h_two, normed_two, factor_two, gains[1])
    grad_resid = upstream_f + grad_resid_norm
    grad_att = of_chip(grad_resid.astype(BF))
    grad_attn = dot(grad_att, w_o).astype(BF)

    grad_query, *kv_terms = attend_back(
        chips, bounds, ranges, query, grad_attn, attn_f, lse, kv_all, scale
    )
    grad_kv = sum_plane(kv_terms).astype(BF)
    grad_qkv = jnp.concatenate([grad_query, grad_kv], axis=1)
    grad_h_one = summed_for_own(times_transposed(grad_qkv, w_qkv))
    grad_input_norm, gain_one_part = norm_backward(grad_h_one, normed_one, factor_one, gains[0])
    input_grad = grad_resid + grad_input_norm

    grads_rest = jnp.concatenate(
        [row_major(transposed_times(grad_att, attn).astype(BF)), shared_grads], axis=1
    )
    rest_sum = lax.psum_scatter(grads_rest, CHIPS, scatter_dimension=0, tiled=True)
    quarter = width // 4
    out_terms = unpick_rows(pick, gate_slot + zero_after(grad_kv), *outs)
    qkv_sum = sum_plane(
        [
            transposed_times(h_one_turned[:, k * quarter : (k + 1) * quarter], grad_qkv).astype(BF)
            for k in range(4)
        ],
        zero_after(out_terms[0]),
    )
    mixture = sum_plane(out_terms)
    block_out = (resid + shared_out + mixture).astype(BF)
    part_sum = jnp.concatenate([qkv_sum.astype(BF), rest_sum], axis=1)
    blocks = lax.all_to_all(
        part_sum.reshape(8, chip_rows // 8, MINE), COLUMN, 0, 0, tiled=True
    ).reshape(2, 4, chip_rows // 8, MINE)
    dense_grad = whole_of(
        jnp.sum(blocks[..., :QKVO_HALF].astype(F32), axis=1), blocks[..., QKVO_HALF:].astype(F32)
    )

    gain_part = jnp.stack([gain_one_part, gain_two_part])
    local_squares = jnp.sum(dense_grad * dense_grad) + jnp.sum(expert_grad * expert_grad)
    gain_tiles = gain_part.size // 128
    packed = jnp.concatenate(
        [
            gain_part.reshape(gain_tiles, 128),
            jnp.broadcast_to(local_squares, (8, 128)),
        ],
        axis=0,
    )
    packed = total_over_all(packed)
    gain_grad = packed[:gain_tiles].reshape(gain_part.shape)
    total_squares = packed[gain_tiles, 0]
    grad_norm = jnp.sqrt(total_squares + jnp.sum(gain_grad * gain_grad))
    clip_factor = jnp.minimum(1.0, CLIP_NORM / (grad_norm + 1e-06))
    dense_new, dense_first_new, dense_second_new = adamw_step(
        dense_weights,
        dense_first,
        dense_second,
        dense_grad * clip_factor,
        MATRIX_RATE,
        WEIGHT_DECAY,
    )
    expert_new, expert_first_new, expert_second_new = adamw_step(
        expert_weights,
        expert_first,
        expert_second,
        expert_grad[None] * clip_factor,
        MATRIX_RATE,
        WEIGHT_DECAY,
    )
    gain_cols = gain_first.shape[1]
    gain_begin = lax.axis_index(ALL) * gain_cols
    gain_slice = lax.dynamic_slice_in_dim(gains, gain_begin, gain_cols, 1)
    gain_grad_slice = lax.dynamic_slice_in_dim(gain_grad, gain_begin, gain_cols, 1)
    gain_new, gain_first_new, gain_second_new = adamw_step(
        gain_slice, gain_first, gain_second, gain_grad_slice * clip_factor, GAIN_RATE, 0.0
    )
    return (
        block_out[None],
        input_grad[None],
        grad_norm,
        dense_new,
        dense_first_new,
        dense_second_new,
        expert_new,
        expert_first_new,
        expert_second_new,
        gain_new,
        gain_first_new,
        gain_second_new,
    )


def solution(mesh):
    fine = Mesh(mesh.devices.reshape(4, 4, 2, 2, 2), ALL)
    sequence = (DEPTH, CTX)
    token = P(*sequence, None)
    dense = P(ALL, None)
    expert = P(CTX, DEPTH, None)
    gain = P(None, ALL)
    return jax.shard_map(
        shards,
        mesh=fine,
        in_specs=(
            token,
            token,
            P(*sequence),
            token,
            token,
            dense,
            dense,
            dense,
            expert,
            expert,
            expert,
            P(),
            gain,
            gain,
        ),
        out_specs=(
            token,
            token,
            P(),
            dense,
            dense,
            dense,
            expert,
            expert,
            expert,
            gain,
            gain,
            gain,
        ),
        check_vma=False,
    )
```
